32 devices in a mesh: role: 2 (over core), dev: 16 (over z, y, x).
Axes of the slice: x: 2, y: 2, z: 4, core: 2. Of those that a mesh axis runs over, the one named last changes fastest.
Arguments:
- moe_rows: bfloat16 [1024, 3584], P(('role', 'dev')), may hold values from -6 to 6
- expert_ids: int32 [1024, 8], P(('role', 'dev')), may hold values from 0 to 15, all different within a row; in each aligned block of 32 rows (0 to 31, 32 to 63, ...) at most 32 rows name the same one
- gate_weights: float32 [1024, 8], P(('role', 'dev')), may hold values from 0.05 to 0.6
- w_gate: bfloat16 [16, 3584, 1024], P('dev', None, 'role'), may hold values from -0.09375 to 0.09375
- w_up: bfloat16 [16, 3584, 1024], P('dev', None, 'role'), may hold values from -0.09375 to 0.09375
- w_down: bfloat16 [16, 3584, 1024], P('dev', None, 'role'), may hold values from -0.1875 to 0.1875
- q_latent: bfloat16 [128, 64, 512], P(('role', 'dev')), may hold values from -40 to 40
- q_rope: bfloat16 [128, 4096], P(('role', 'dev')), may hold values from -4 to 4
- latent_cache: bfloat16 [128, 2048, 512], P(('role', 'dev')), may hold values from -4 to 4
- rope_cache: bfloat16 [128, 64, 2048], P(('role', 'dev')), may hold values from -4 to 4
- lengths: int32 [128], P(('role', 'dev')), may hold values from 2 to 2048, as said below
Outputs:
- moe_out: bfloat16 [1024, 3584], P(('role', 'dev'))
- attended: bfloat16 [128, 64, 512], P(('role', 'dev'))
The draws below stay inside these ranges and needn't reach their ends.
Inputs may be any that keep to these rules, and one draw needn't show every extreme that they name: `expert_ids`: each row names 8 different experts; among the rows of one device no expert is named more than 32 times. `lengths`: the first row holds all 2048 cached tokens.
All inputs are finite; a program needn't handle non-finite values.
Results may differ from the reference program's by a relative error of at most 0.0057.
Values may be sent and summed in bfloat16 or wider, within the bound.
No kernel may reach another device: no remote copies, remote signals or barrier semaphores. Data moves between devices by JAX's collectives and lax.ppermute only.
A program may use at most 128 MiB of HBM per device.

```python
import math
import jax
import jax.numpy as jnp
import numpy as np
from jax import lax

DW = 3584
FFW = 1024
TOPK = 8
HEADS = 64
LATENT = 512
ROPE = 64
TOK_DEV = 32
CACHE = 2048
EXPERTS = 16
CAP = 32
ROWS_MOE = 1024
ROWS_ATT = 128
N_ROLE = 2
N_DEV = 16


def cache_field(key):
    base = jnp.clip(jax.random.normal(jax.random.fold_in(key, 7), (ROWS_ATT, CACHE, LATENT), jnp.float32), -4.0, 4.0)
    return base


def draw_latent_cache(key, part):
    return cache_field(key).astype(jnp.bfloat16)


def draw_q_latent(key, part):
    result = jnp.clip(jax.random.normal(jax.random.fold_in(key, 19), (ROWS_ATT, HEADS, LATENT), jnp.float32), -4.0, 4.0)
    return result.astype(jnp.bfloat16)


def draw_q_rope(key, part):
    result = jnp.clip(jax.random.normal(jax.random.fold_in(key, 23), (ROWS_ATT, HEADS * ROPE), jnp.float32), -4.0, 4.0)
    return result.astype(jnp.bfloat16)


def draw_lengths(key, part):
    drawn = jax.random.randint(jax.random.fold_in(key, 29), (ROWS_ATT,), 2, CACHE + 1, jnp.int32)
    return jnp.where(jnp.arange(ROWS_ATT) == 0, CACHE, drawn).astype(jnp.int32)


def steps_of(key, extent, split, smallest, high):
    loudness, own = 1.0, jax.random.fold_in(key, 6)
    for axis_at, parts in split:
        draws = jnp.exp(jax.random.uniform(jax.random.fold_in(own, axis_at), (parts,), jnp.float32, smallest / len(split), high / len(split)))
        loudness = loudness * jnp.repeat(draws, extent[axis_at] // parts).reshape([-1 if axis == axis_at else 1 for axis in range(len(extent))])
    return loudness


def deal_out(own_key, own, number, rows, amount, top, most, skew):
    order = jax.random.permutation(own_key, amount)
    packed, usual = portions_of(amount, rows * top, most, skew, True), portions_of(amount, rows * top, most, skew, False)
    places = jnp.arange(amount)

    def named(sizes, offset_by):
        used = int((sizes > 0).sum())
        fixed = max(1, used // 4)
        passed = fixed + (places - fixed + offset_by * (used - fixed)) % max(1, amount - fixed)
        return jnp.zeros((amount,), jnp.int32).at[order[jnp.where(places < fixed, places, passed)]].set(jnp.asarray(sizes, jnp.int32))

    sizes = jnp.where(number % 4 == 0, named(packed, number // 4), named(usual, number - number // 4 - 1))
    mixed = jax.random.permutation(jax.random.fold_in(own, 3), amount)
    giver, taker = mixed[0:amount // 2 * 2:2], mixed[1:amount // 2 * 2:2]
    margin = jnp.minimum(sizes[giver] - 1, most - sizes[taker]) // 2
    margin = jnp.where((giver == order[0]) | (taker == order[0]) | (sizes[taker] == 0), 0, jnp.maximum(margin, 0))
    passed = jax.random.randint(jax.random.fold_in(own, 4), (amount // 2,), 0, 1 << 20) % (margin + 1)
    sizes = sizes.at[giver].add(-passed).at[taker].add(passed)
    items = jnp.searchsorted(jnp.cumsum(sizes), jnp.arange(rows * top), side="right").astype(jnp.int32)
    table = items.reshape(top, rows).T
    table = table[jax.random.permutation(jax.random.fold_in(own, 1), rows)]
    offset_by = jax.random.randint(jax.random.fold_in(own, 2), (rows, 1), 0, top)
    return jnp.take_along_axis(table, (jnp.arange(top)[None, :] + offset_by) % top, axis=1)


def portions_of(amount, total, reach, slope, full):
    loads = [(1 << 20) // math.isqrt(grade ** slope) + 1 for grade in range(1, amount + 1)]
    largest = reach if full else min(reach, max(-(-total // amount), total * loads[0] // sum(loads)))
    least = 1 if total - largest >= amount - 1 else 0
    given, surplus = [largest] + [least] * (amount - 1), total - largest - least * (amount - 1)
    while surplus > 0:
        movable = [i for i in range(1, amount) if given[i] < largest] or [i for i in range(1, amount) if given[i] < reach]
        whole, remaining = sum([loads[i] for i in movable]), surplus
        for i in movable:
            extra = min(reach - given[i], max(1, remaining * loads[i] // whole), surplus)
            given[i] = given[i] + extra
            surplus = surplus - extra
    return np.array(given)


def gaussian(rng, extent, spread, most, shards=(), kind=jnp.bfloat16):
    array = jax.random.normal(rng, extent, jnp.float32) * spread
    if len(shards) > 0:
        array = steps_of(rng, extent, shards, -0.22, 0.18) * array
    return jnp.clip(array, min=-most, max=most).astype(kind)


def setup_inputs(seed: int = 0) -> dict:
    key_list = jax.random.split(jax.random.key(seed), 12)
    moe_rows = gaussian(key_list[0], (ROWS_MOE, DW), 1.0, 6.0, ((0, 32),))
    expert_ids_keys = jax.random.split(jax.random.fold_in(key_list[1], 1), ROWS_MOE // TOK_DEV)
    expert_ids_turns = jax.random.permutation(jax.random.fold_in(key_list[1], 3), ROWS_MOE // TOK_DEV)
    expert_ids = jax.vmap(lambda own, number: deal_out(jax.random.fold_in(key_list[1], 2), own, number, TOK_DEV, EXPERTS, TOPK, CAP, 2))(expert_ids_keys, expert_ids_turns).reshape((ROWS_MOE, TOPK))
    gate_weights = jnp.clip(0.05 + 0.55 * jax.random.uniform(key_list[2], (ROWS_MOE, TOPK), jnp.float32) ** steps_of(key_list[2], (ROWS_MOE, TOPK), ((0, 32),), -0.2, 0.2), 0.05, 0.6)
    w_gate = gaussian(key_list[3], (EXPERTS, DW, FFW), DW ** -0.5, 0.09375, ((0, 16), (2, 2)))
    w_up = gaussian(key_list[4], (EXPERTS, DW, FFW), DW ** -0.5, 0.09375, ((0, 16), (2, 2)))
    w_down = gaussian(key_list[5], (EXPERTS, DW, FFW), FFW ** -0.5, 0.1875, ((0, 16), (2, 2)))
    q_latent = draw_q_latent(jax.random.fold_in(key_list[11], 71), 0)
    q_rope = draw_q_rope(jax.random.fold_in(key_list[11], 71), 0)
    latent_cache = draw_latent_cache(jax.random.fold_in(key_list[11], 71), 0)
    rope_cache = gaussian(key_list[9], (ROWS_ATT, ROPE, CACHE), 1.0, 4.0, ((0, 32),))
    lengths = draw_lengths(jax.random.fold_in(key_list[11], 71), 0)
    return {"moe_rows": moe_rows, "expert_ids": expert_ids, "gate_weights": gate_weights, "w_gate": w_gate, "w_up": w_up, "w_down": w_down, "q_latent": q_latent, "q_rope": q_rope, "latent_cache": latent_cache, "rope_cache": rope_cache, "lengths": lengths}


score_scale = 192.0 ** -0.5


def expert_block(chosen, gate_matrix, up_matrix, down_matrix):
    gate_part = jnp.dot(chosen, gate_matrix, preferred_element_type=jnp.float32)
    up_part = jnp.dot(chosen, up_matrix, preferred_element_type=jnp.float32)
    hidden_units = (jax.nn.silu(gate_part) * up_part).astype(jnp.bfloat16)
    return lax.dot_general(hidden_units, down_matrix, (((1,), (1,)), ((), ())), preferred_element_type=jnp.float32)


def attend_row(operands):
    query_lat, query_rope, cache_lat, cache_rope, length = operands
    head_count = query_lat.shape[0]
    rope_width = cache_rope.shape[0]
    scores = lax.dot_general(query_lat, cache_lat, (((1,), (1,)), ((), ())), preferred_element_type=jnp.float32)
    scores = scores + jnp.dot(query_rope.reshape(head_count, rope_width), cache_rope, preferred_element_type=jnp.float32)
    scores = scores * score_scale
    positions = jnp.arange(cache_lat.shape[0], dtype=jnp.int32)
    valid = (positions < length)[None, :]
    scores = jnp.where(valid, scores, jnp.float32(-1e30))
    highest = jnp.max(scores, axis=1, keepdims=True)
    weights = jnp.where(valid, jnp.exp(scores - highest), jnp.float32(0.0))
    probs = (weights / jnp.sum(weights, axis=1, keepdims=True)).astype(jnp.bfloat16)
    return jnp.dot(probs, cache_lat, preferred_element_type=jnp.float32).astype(jnp.bfloat16)


def reference(moe_rows, expert_ids, gate_weights, w_gate, w_up, w_down, q_latent, q_rope, latent_cache, rope_cache, lengths):
    flat_ids = expert_ids.reshape(-1)
    pair_count = flat_ids.shape[0]
    width = moe_rows.shape[1]
    padded_rows = jnp.concatenate([moe_rows, jnp.zeros((1, width), jnp.bfloat16)], axis=0)
    flat_gates = jnp.concatenate([gate_weights.reshape(-1), jnp.zeros((1,), jnp.float32)], axis=0)
    bound = N_ROLE * N_DEV * CAP

    def per_expert(running, expert):
        picks = jnp.nonzero(flat_ids == expert, size=bound, fill_value=pair_count)[0].astype(jnp.int32)
        row_index = jnp.where(picks < pair_count, picks // TOPK, ROWS_MOE).astype(jnp.int32)
        chosen = padded_rows[row_index]
        result = expert_block(chosen, w_gate[expert], w_up[expert], w_down[expert]).astype(jnp.bfloat16)
        result = lax.optimization_barrier(result).astype(jnp.float32)
        weighted = result * flat_gates[picks][:, None]
        return running.at[row_index].add(weighted), None

    start_sum = jnp.zeros((ROWS_MOE + 1, width), jnp.float32)
    running, _ = lax.scan(per_expert, start_sum, jnp.arange(EXPERTS, dtype=jnp.int32))
    moe_out = running[:ROWS_MOE].astype(jnp.bfloat16)
    attended = lax.map(attend_row, (q_latent, q_rope, latent_cache, rope_cache, lengths))
    return (moe_out, attended)
```

```python
import functools

import jax
import jax.numpy as jnp
from jax import lax
from jax.experimental import pallas as pl
from jax.experimental.pallas import tpu as pltpu
from jax.sharding import PartitionSpec as P

score_scale = 192.0 ** (-0.5)
both_axes = ("role", "dev")
chunk_count = 2


def shift_pairs(kind, step, depth, side):
    pairs = []
    for r in range(2):
        for z in range(depth):
            for y in range(side):
                for x in range(side):
                    to_r, to_z, to_y, to_x = r, z, y, x
                    if kind == "role":
                        to_r = 1 - r
                    elif kind == "z":
                        to_z = (z + step) % depth
                    elif (kind == "first") == (r == 0):
                        to_y = (y + step) % side
                    else:
                        to_x = (x + step) % side
                    here = ((r * depth + z) * side + y) * side + x
                    there = ((to_r * depth + to_z) * side + to_y) * side + to_x
                    pairs.append((here, there))
    return pairs


def attend_row(query_lat, query_rope, cache_lat, cache_rope, length):
    head_count = query_lat.shape[0]
    rope_width = cache_rope.shape[0]
    scores = lax.dot_general(
        query_lat, cache_lat, (((1,), (1,)), ((), ())), preferred_element_type=jnp.float32
    )
    scores = scores + jnp.dot(
        query_rope.reshape(head_count, rope_width), cache_rope, preferred_element_type=jnp.float32
    )
    scores = scores * score_scale
    positions = jnp.arange(cache_lat.shape[0], dtype=jnp.int32)
    valid = (positions < length)[None, :]
    scores = jnp.where(valid, scores, jnp.float32(-1e30))
    highest = jnp.max(scores, axis=1, keepdims=True)
    weights = jnp.where(valid, jnp.exp(scores - highest), jnp.float32(0.0))
    probs = (weights / jnp.sum(weights, axis=1, keepdims=True)).astype(jnp.bfloat16)
    return jnp.dot(probs, cache_lat, preferred_element_type=jnp.float32).astype(jnp.bfloat16)


def expert_kernel(count, lane_ref, *refs):
    blocks, refs = refs[:count], refs[count:]
    (gate_mat, up_mat, down_mat), refs = refs[:3], refs[3:]
    results, refs = refs[:count], refs[count:]
    rows, hidden, finished, in_sem, out_sem = refs
    block = blocks[0].shape[0]
    width, units = gate_mat.shape
    together = max(1, min(count, 256 // block))
    slab = width // 2

    def load(at):
        return pltpu.make_async_copy(
            blocks[at], rows.at[pl.ds(at * block, block)], in_sem.at[at]
        )

    def store(at):
        return pltpu.make_async_copy(
            finished.at[pl.ds(at * block, block)], results[at], out_sem.at[at]
        )

    for at in range(count):
        load(at).start()
    for first in range(0, count, together):
        group = range(first, first + together)
        for at in group:
            load(at).wait()
        cut = pl.ds(first * block, together * block)
        row_gates = jnp.sum(
            rows[cut, width:].astype(jnp.float32) * lane_ref[...], axis=1, keepdims=True
        )
        chosen = rows[cut, :width]
        gate_part = jnp.dot(chosen, gate_mat[...], preferred_element_type=jnp.float32)
        up_part = jnp.dot(chosen, up_mat[...], preferred_element_type=jnp.float32)
        silu = gate_part / (1.0 + jnp.exp(-gate_part))
        hidden[cut] = (silu * up_part).astype(jnp.bfloat16)
        for piece in range(2):
            lanes = pl.ds(piece * slab, slab)
            result = lax.dot_general(
                hidden[cut],
                down_mat[lanes, :],
                (((1,), (1,)), ((), ())),
                preferred_element_type=jnp.float32,
            )
            finished[cut, lanes] = (result * row_gates).astype(jnp.bfloat16)
        for at in group:
            store(at).start()
    for at in range(count):
        store(at).wait()


def expert_blocks(blocks, gate_matrix, up_matrix, down_matrix, own_lane):
    count = len(blocks)
    block, padded = blocks[0].shape
    width, units = gate_matrix.shape
    total = count * block
    anywhere = pl.BlockSpec(memory_space=pl.ANY)
    inside = pl.BlockSpec(memory_space=pltpu.VMEM)
    return pl.pallas_call(
        functools.partial(expert_kernel, count),
        out_shape=[jax.ShapeDtypeStruct((block, width), jnp.bfloat16)] * count,
        in_specs=[inside] + [anywhere] * count + [inside] * 3,
        out_specs=[anywhere] * count,
        scratch_shapes=[
            pltpu.VMEM((total, padded), jnp.bfloat16),
            pltpu.VMEM((total, units), jnp.bfloat16),
            pltpu.VMEM((total, width), jnp.bfloat16),
            pltpu.SemaphoreType.DMA((count,)),
            pltpu.SemaphoreType.DMA((count,)),
        ],
        compiler_params=pltpu.CompilerParams(vmem_limit_bytes=24 * 1024 * 1024),
        cost_estimate=pl.CostEstimate(
            flops=6 * total * width * units,
            bytes_accessed=6 * width * units + 4 * total * width,
            transcendentals=total * units,
        ),
        name="expert_blocks",
    )(own_lane, *blocks, gate_matrix, up_matrix, down_matrix)


def after(value, *earlier):
    return lax.optimization_barrier((value, *earlier))[0]


def per_device(
    moe_rows,
    expert_ids,
    gate_weights,
    w_gate,
    w_up,
    w_down,
    q_latent,
    q_rope,
    latent_cache,
    rope_cache,
    lengths,
):
    tok_count, width = moe_rows.shape
    experts = lax.axis_size("dev")
    side = 1
    while experts % (4 * side * side) == 0 and (2 * side) ** 2 * 4 <= experts:
        side *= 2
    depth = experts // (side * side)
    chunk = tok_count // chunk_count
    block = depth * chunk

    def send(value, kind, step=1):
        return lax.ppermute(value, both_axes, shift_pairs(kind, step, depth, side))

    place = lax.axis_index("dev")
    named = expert_ids[:, :, None] == jnp.arange(experts, dtype=jnp.int32)[None, None, :]
    dense_gates = jnp.sum(jnp.where(named, gate_weights[:, :, None], 0.0), axis=1)
    kept_part = lax.reduce_precision(dense_gates, exponent_bits=8, mantissa_bits=7)
    upper = kept_part.astype(jnp.bfloat16)
    lower = (dense_gates - kept_part).astype(jnp.bfloat16)
    spare = -(2 * experts) % 128
    tail = jnp.concatenate([upper, lower, jnp.zeros((tok_count, spare), jnp.bfloat16)], axis=1)
    tail_width = tail.shape[1]
    payload = jnp.concatenate([moe_rows, tail], axis=1)
    lane = jnp.arange(tail_width, dtype=jnp.int32)
    own_lane = ((lane == place) | (lane == place + experts)).astype(jnp.float32)[None, :]

    gathered = []
    line = None
    for c in range(chunk_count):
        mine = payload[c * chunk : (c + 1) * chunk]
        if line is not None:
            mine = after(mine, line)
        line = jnp.concatenate([mine] + [send(mine, "z", k) for k in range(1, depth)], axis=0)
        first = [line] + [send(line, "first", k) for k in range(1, side)]
        blocks = list(first)
        for k in range(1, side):
            blocks += [send(part, "last", k) for part in first]
        gathered.append(blocks + [send(part, "role") for part in blocks])

    finished = []
    summed = None
    for c in range(chunk_count):
        results = []
        for at in range(0, len(gathered[c]), 8):
            group = gathered[c][at : at + 8]
            if summed is not None:
                group = [after(group[0], summed)] + group[1:]
            results += expert_blocks(group, w_gate[0], w_up[0], w_down[0], own_lane)
        half = len(results) // 2
        whole = [
            (mine.astype(jnp.float32) + send(yours, "role").astype(jnp.float32))
            for mine, yours in zip(results[:half], results[half:])
        ]
        whole = [whole[k * side : (k + 1) * side] for k in range(side)]
        sent = [[part.astype(jnp.bfloat16) for part in row] for row in whole]
        summed = sent[side - 1][side - 1]
        kept = {}
        for a in reversed(range(side)):
            total = whole[0][a]
            for k in range(1, side):
                total = total + send(sent[k][a], "last", -k).astype(jnp.float32)
            kept[a] = total
        total = kept[0]
        for k in range(1, side):
            total = total + send(kept[k].astype(jnp.bfloat16), "first", -k).astype(jnp.float32)
        line = total.astype(jnp.bfloat16).reshape(depth, chunk, width)
        total = line[0].astype(jnp.float32)
        for k in range(1, depth):
            total = total + send(line[k], "z", -k).astype(jnp.float32)
        finished.append(total.astype(jnp.bfloat16))
    moe_out = jnp.concatenate(finished, axis=0)
    attended = jax.vmap(attend_row)(q_latent, q_rope, latent_cache, rope_cache, lengths)
    return (moe_out, attended)


def solution(mesh):
    placed = (
        P(("role", "dev"), None),
        P(("role", "dev"), None),
        P(("role", "dev"), None),
        P("dev", None, "role"),
        P("dev", None, "role"),
        P("dev", None, "role"),
        P(("role", "dev"), None, None),
        P(("role", "dev"), None),
        P(("role", "dev"), None, None),
        P(("role", "dev"), None, None),
        P(("role", "dev")),
    )
    return jax.shard_map(
        per_device,
        mesh=mesh,
        in_specs=placed,
        out_specs=(P(("role", "dev"), None), P(("role", "dev"), None, None)),
        check_vma=False,
    )
```

```python
import functools

import jax
import jax.numpy as jnp
from jax import lax
from jax.experimental import pallas as pl
from jax.experimental.pallas import tpu as pltpu
from jax.sharding import PartitionSpec as P

score_scale = 192.0 ** (-0.5)
both_axes = ("role", "dev")
chunk_count = 2


def shift_pairs(kind, step, depth, side):
    pairs = []
    for r in range(2):
        for z in range(depth):
            for y in range(side):
                for x in range(side):
                    to_r, to_z, to_y, to_x = r, z, y, x
                    if kind == "role":
                        to_r = 1 - r
                    elif kind == "z":
                        to_z = (z + step) % depth
                    elif (kind == "first") == (r == 0):
                        to_y = (y + step) % side
                    else:
                        to_x = (x + step) % side
                    here = ((r * depth + z) * side + y) * side + x
                    there = ((to_r * depth + to_z) * side + to_y) * side + to_x
                    pairs.append((here, there))
    return pairs


def attend_kernel(lengths_ref, lat_ref, rope_ref, cache_ref, keys_ref, *refs):
    out_ref = refs[-1]
    length = lengths_ref[pl.program_id(0)]
    cache = cache_ref[0]
    scores = lax.dot_general(
        lat_ref[0], cache, (((1,), (1,)), ((), ())), preferred_element_type=jnp.float32
    )
    scores = scores + jnp.dot(rope_ref[0], keys_ref[0], preferred_element_type=jnp.float32)
    scores = scores * score_scale
    valid = lax.broadcasted_iota(jnp.int32, scores.shape, 1) < length
    scores = jnp.where(valid, scores, jnp.float32(-1e30))
    highest = jnp.max(scores, axis=1, keepdims=True)
    weights = jnp.where(valid, jnp.exp(scores - highest), jnp.float32(0.0))
    probs = weights * (1.0 / jnp.sum(weights, axis=1, keepdims=True))
    out_ref[0] = jnp.dot(
        probs.astype(jnp.bfloat16), cache, preferred_element_type=jnp.float32
    ).astype(jnp.bfloat16)


def attend_rows(q_latent, q_rope, latent_cache, rope_cache, lengths, start, count, resident=()):
    heads, latent = q_latent.shape[1:]
    cached = latent_cache.shape[1]
    rope = rope_cache.shape[1]

    def spec(*shape):
        return pl.BlockSpec((1, *shape), lambda at, lengths_ref: (start + at, 0, 0))

    return pl.pallas_call(
        attend_kernel,
        out_shape=jax.ShapeDtypeStruct((count, heads, latent), jnp.bfloat16),
        grid_spec=pltpu.PrefetchScalarGridSpec(
            num_scalar_prefetch=1,
            grid=(count,),
            in_specs=[
                spec(heads, latent),
                spec(heads, rope),
                spec(cached, latent),
                spec(rope, cached),
            ]
            + [pl.BlockSpec(memory_space=pltpu.VMEM)] * len(resident),
            out_specs=pl.BlockSpec((1, heads, latent), lambda at, lengths_ref: (at, 0, 0)),
        ),
        compiler_params=pltpu.CompilerParams(vmem_limit_bytes=(46 if resident else 48) * 1024 * 1024),
        cost_estimate=pl.CostEstimate(
            flops=2 * count * heads * cached * (2 * latent + rope),
            bytes_accessed=2 * count * cached * (latent + rope),
            transcendentals=count * heads * cached,
        ),
        name="attend_rows",
    )(lengths[start : start + count], q_latent, q_rope, latent_cache, rope_cache, *resident)


def expert_kernel(count, lane_ref, *refs):
    blocks, refs = refs[:count], refs[count:]
    (gate_mat, up_mat, down_mat), refs = refs[:3], refs[3:]
    results, (hidden,) = refs[:count], refs[count:]
    block = blocks[0].shape[0]
    width, units = gate_mat.shape
    tile, slab = units // 2, width // 2
    chosen = jnp.concatenate([rows[:, :width] for rows in blocks], axis=0)
    tails = jnp.concatenate([rows[:, width:] for rows in blocks], axis=0)
    row_gates = jnp.sum(tails.astype(jnp.float32) * lane_ref[...], axis=1, keepdims=True)
    for piece in range(2):
        lanes = pl.ds(piece * tile, tile)
        gate_part = jnp.dot(chosen, gate_mat[:, lanes], preferred_element_type=jnp.float32)
        up_part = jnp.dot(chosen, up_mat[:, lanes], preferred_element_type=jnp.float32)
        silu = gate_part / (1.0 + jnp.exp(-gate_part))
        hidden[:, lanes] = (silu * up_part).astype(jnp.bfloat16)
    for piece in range(2):
        lanes = pl.ds(piece * slab, slab)
        result = lax.dot_general(
            hidden[...],
            down_mat[lanes, :],
            (((1,), (1,)), ((), ())),
            preferred_element_type=jnp.float32,
        )
        result = (result * row_gates).astype(jnp.bfloat16)
        for at in range(count):
            results[at][:, lanes] = result[at * block : (at + 1) * block]


def expert_blocks(blocks, gate_matrix, up_matrix, down_matrix, own_lane):
    count = len(blocks)
    block = blocks[0].shape[0]
    width, units = gate_matrix.shape
    total = count * block
    inside = pl.BlockSpec(memory_space=pltpu.VMEM)
    return pl.pallas_call(
        functools.partial(expert_kernel, count),
        out_shape=[jax.ShapeDtypeStruct((block, width), jnp.bfloat16)] * count,
        in_specs=[inside] * (count + 4),
        out_specs=[inside] * count,
        scratch_shapes=[pltpu.VMEM((total, units), jnp.bfloat16)],
        compiler_params=pltpu.CompilerParams(vmem_limit_bytes=10 * 1024 * 1024),
        cost_estimate=pl.CostEstimate(
            flops=6 * total * width * units,
            bytes_accessed=6 * width * units + 4 * total * width,
            transcendentals=total * units,
        ),
        name="expert_blocks",
    )(own_lane, *blocks, gate_matrix, up_matrix, down_matrix)


def after(value, *earlier):
    return lax.optimization_barrier((value, *earlier))[0]


def per_device(
    moe_rows,
    expert_ids,
    gate_weights,
    w_gate,
    w_up,
    w_down,
    q_latent,
    q_rope,
    latent_cache,
    rope_cache,
    lengths,
):
    tok_count, width = moe_rows.shape
    experts = lax.axis_size("dev")
    side = 1
    while experts % (4 * side * side) == 0 and (2 * side) ** 2 * 4 <= experts:
        side *= 2
    depth = experts // (side * side)
    chunk = tok_count // chunk_count
    block = depth * chunk

    def send(value, kind, step=1):
        return lax.ppermute(value, both_axes, shift_pairs(kind, step, depth, side))

    place = lax.axis_index("dev")
    named = expert_ids[:, :, None] == jnp.arange(experts, dtype=jnp.int32)[None, None, :]
    dense_gates = jnp.sum(jnp.where(named, gate_weights[:, :, None], 0.0), axis=1)
    kept_part = lax.reduce_precision(dense_gates, exponent_bits=8, mantissa_bits=7)
    upper = kept_part.astype(jnp.bfloat16)
    lower = (dense_gates - kept_part).astype(jnp.bfloat16)
    spare = -(2 * experts) % 128
    tail = jnp.concatenate([upper, lower, jnp.zeros((tok_count, spare), jnp.bfloat16)], axis=1)
    tail_width = tail.shape[1]
    payload = jnp.concatenate([moe_rows, tail], axis=1)
    lane = jnp.arange(tail_width, dtype=jnp.int32)
    own_lane = ((lane == place) | (lane == place + experts)).astype(jnp.float32)[None, :]
    payload = after(payload, own_lane)

    att_rows = lengths.shape[0]
    rope_rows = q_rope.reshape(att_rows, q_latent.shape[1], rope_cache.shape[1])
    att_half = att_rows // 2

    matrices = (w_gate[0], w_up[0], w_down[0])

    def attend(start, key, resident=()):
        return attend_rows(
            q_latent, key, latent_cache, rope_cache, lengths, start, att_half, resident
        )

    def pieces(c):
        return payload[c * chunk : (c + 1) * chunk]

    def along(mine):
        return [mine] + [send(mine, "z", k) for k in range(1, depth)]

    early = attend(0, rope_rows)
    gathered = []
    coming = along(pieces(0))
    coming[1] = after(coming[1], early)
    last = None
    for c in range(chunk_count):
        line = jnp.concatenate(coming, axis=0)
        if last is not None:
            line = after(line, last)
        if c + 1 < chunk_count:
            coming = along(after(pieces(c + 1), line))
        first = [line] + [send(line, "first", k) for k in range(1, side)]
        if c == 0:
            late = attend(att_half, after(rope_rows, line))
            first[1] = after(first[1], late, *coming)
        blocks = list(first)
        for k in range(1, side):
            blocks += [send(part, "last", k) for part in first]
        last = blocks[-1]
        gathered.append(blocks + [send(part, "role") for part in blocks])

    finished = []
    summed = None
    for c in range(chunk_count):
        half = len(gathered[c]) // 2
        own, other = gathered[c][:half], gathered[c][half:]
        if summed is not None:
            other = [after(other[0], summed)] + other[1:]

        def expert(blocks):
            results = []
            for at in range(0, half, 4):
                results += expert_blocks(blocks[at : at + 4], *matrices, own_lane)
            return results

        theirs = [send(part, "role") for part in expert(other)]
        if c + 1 < chunk_count:
            following = gathered[c + 1]
            own = [after(own[0], following[1], following[side])] + own[1:]
        mine = expert(own)
        whole = [a.astype(jnp.float32) + b.astype(jnp.float32) for a, b in zip(mine, theirs)]
        whole = [whole[k * side : (k + 1) * side] for k in range(side)]
        sent = [[part.astype(jnp.bfloat16) for part in row] for row in whole]
        summed = sent[side - 1][side - 1]
        kept = {}
        for a in reversed(range(side)):
            total = whole[0][a]
            for k in range(1, side):
                total = total + send(sent[k][a], "last", -k).astype(jnp.float32)
            kept[a] = total
        total = kept[0]
        for k in range(1, side):
            total = total + send(kept[k].astype(jnp.bfloat16), "first", -k).astype(jnp.float32)
        line = total.astype(jnp.bfloat16).reshape(depth, chunk, width)
        total = line[0].astype(jnp.float32)
        for k in range(1, depth):
            total = total + send(line[k], "z", -k).astype(jnp.float32)
        finished.append(total.astype(jnp.bfloat16))
    moe_out = jnp.concatenate(finished, axis=0)
    attended = jnp.concatenate([early, late], axis=0)
    return (moe_out, attended)


def solution(mesh):
    placed = (
        P(("role", "dev"), None),
        P(("role", "dev"), None),
        P(("role", "dev"), None),
        P("dev", None, "role"),
        P("dev", None, "role"),
        P("dev", None, "role"),
        P(("role", "dev"), None, None),
        P(("role", "dev"), None),
        P(("role", "dev"), None, None),
        P(("role", "dev"), None, None),
        P(("role", "dev")),
    )
    return jax.shard_map(
        per_device,
        mesh=mesh,
        in_specs=placed,
        out_specs=(P(("role", "dev"), None), P(("role", "dev"), None, None)),
        check_vma=False,
    )
```

```python
import functools

import jax
import jax.numpy as jnp
from jax import lax
from jax.experimental import pallas as pl
from jax.experimental.pallas import tpu as pltpu
from jax.sharding import PartitionSpec as P

score_scale = 192.0 ** (-0.5)
both_axes = ("role", "dev")
chunk_count = 2


def shift_pairs(kind, step, depth, side):
    pairs = []
    for r in range(2):
        for z in range(depth):
            for y in range(side):
                for x in range(side):
                    to_r, to_z, to_y, to_x = r, z, y, x
                    if kind == "role":
                        to_r = 1 - r
                    elif kind == "z":
                        to_z = z ^ step
                    elif (kind == "first") == (r == 0):
                        to_y = y ^ step
                    else:
                        to_x = x ^ step
                    here = ((r * depth + z) * side + y) * side + x
                    there = ((to_r * depth + to_z) * side + to_y) * side + to_x
                    pairs.append((here, there))
    return pairs


def attend_kernel(lengths_ref, lat_ref, rope_ref, cache_ref, keys_ref, out_ref):
    length = lengths_ref[pl.program_id(0)]
    cache = cache_ref[0]
    scores = lax.dot_general(
        lat_ref[0], cache, (((1,), (1,)), ((), ())), preferred_element_type=jnp.float32
    )
    scores = scores + jnp.dot(rope_ref[0], keys_ref[0], preferred_element_type=jnp.float32)
    scores = scores * score_scale
    valid = lax.broadcasted_iota(jnp.int32, scores.shape, 1) < length
    scores = jnp.where(valid, scores, jnp.float32(-1e30))
    highest = jnp.max(scores, axis=1, keepdims=True)
    weights = jnp.where(valid, jnp.exp(scores - highest), jnp.float32(0.0))
    probs = weights * (1.0 / jnp.sum(weights, axis=1, keepdims=True))
    out_ref[0] = jnp.dot(
        probs.astype(jnp.bfloat16), cache, preferred_element_type=jnp.float32
    ).astype(jnp.bfloat16)


def attend_rows(q_latent, q_rope, latent_cache, rope_cache, lengths, start, count):
    heads, latent = q_latent.shape[1:]
    cached = latent_cache.shape[1]
    rope = rope_cache.shape[1]

    def spec(*shape):
        return pl.BlockSpec((1, *shape), lambda at, lengths_ref: (start + at, 0, 0))

    return pl.pallas_call(
        attend_kernel,
        out_shape=jax.ShapeDtypeStruct((count, heads, latent), jnp.bfloat16),
        grid_spec=pltpu.PrefetchScalarGridSpec(
            num_scalar_prefetch=1,
            grid=(count,),
            in_specs=[
                spec(heads, latent),
                spec(heads, rope),
                spec(cached, latent),
                spec(rope, cached),
            ],
            out_specs=pl.BlockSpec((1, heads, latent), lambda at, lengths_ref: (at, 0, 0)),
        ),
        compiler_params=pltpu.CompilerParams(vmem_limit_bytes=48 * 1024 * 1024),
        cost_estimate=pl.CostEstimate(
            flops=2 * count * heads * cached * (2 * latent + rope),
            bytes_accessed=2 * count * cached * (latent + rope),
            transcendentals=count * heads * cached,
        ),
        name="attend_rows",
    )(lengths[start : start + count], q_latent, q_rope, latent_cache, rope_cache)


def expert_kernel(count, lane_ref, *refs):
    blocks, refs = refs[:count], refs[count:]
    (gate_mat, up_mat, down_mat), refs = refs[:3], refs[3:]
    results, (hidden,) = refs[:count], refs[count:]
    block = blocks[0].shape[0]
    width, units = gate_mat.shape
    tile, slab = units // 2, width // 2
    chosen = jnp.concatenate([rows[:, :width] for rows in blocks], axis=0)
    tails = jnp.concatenate([rows[:, width:] for rows in blocks], axis=0)
    row_gates = jnp.sum(tails.astype(jnp.float32) * lane_ref[...], axis=1, keepdims=True)
    for piece in range(2):
        lanes = pl.ds(piece * tile, tile)
        gate_part = jnp.dot(chosen, gate_mat[:, lanes], preferred_element_type=jnp.float32)
        up_part = jnp.dot(chosen, up_mat[:, lanes], preferred_element_type=jnp.float32)
        silu = gate_part / (1.0 + jnp.exp(-gate_part))
        hidden[:, lanes] = (silu * up_part).astype(jnp.bfloat16)
    for piece in range(2):
        lanes = pl.ds(piece * slab, slab)
        result = lax.dot_general(
            hidden[...],
            down_mat[lanes, :],
            (((1,), (1,)), ((), ())),
            preferred_element_type=jnp.float32,
        )
        result = (result * row_gates).astype(jnp.bfloat16)
        for at in range(count):
            results[at][:, lanes] = result[at * block : (at + 1) * block]


def expert_blocks(blocks, gate_matrix, up_matrix, down_matrix, own_lane):
    count = len(blocks)
    block = blocks[0].shape[0]
    width, units = gate_matrix.shape
    total = count * block
    inside = pl.BlockSpec(memory_space=pltpu.VMEM)
    return pl.pallas_call(
        functools.partial(expert_kernel, count),
        out_shape=[jax.ShapeDtypeStruct((block, width), jnp.bfloat16)] * count,
        in_specs=[inside] * (count + 4),
        out_specs=[inside] * count,
        scratch_shapes=[pltpu.VMEM((total, units), jnp.bfloat16)],
        compiler_params=pltpu.CompilerParams(vmem_limit_bytes=10 * 1024 * 1024),
        cost_estimate=pl.CostEstimate(
            flops=6 * total * width * units,
            bytes_accessed=6 * width * units + 4 * total * width,
            transcendentals=total * units,
        ),
        name="expert_blocks",
    )(own_lane, *blocks, gate_matrix, up_matrix, down_matrix)


def after(value, *earlier):
    return lax.optimization_barrier((value, *earlier))[0]


def per_device(
    moe_rows,
    expert_ids,
    gate_weights,
    w_gate,
    w_up,
    w_down,
    q_latent,
    q_rope,
    latent_cache,
    rope_cache,
    lengths,
):
    tok_count, width = moe_rows.shape
    experts = lax.axis_size("dev")
    side = 1
    while experts % (4 * side * side) == 0 and (2 * side) ** 2 * 4 <= experts:
        side *= 2
    depth = experts // (side * side)
    chunk = tok_count // chunk_count
    block = depth * chunk

    def send(value, kind, step=1):
        return lax.ppermute(value, both_axes, shift_pairs(kind, step, depth, side))

    place = lax.axis_index("dev")
    named = expert_ids[:, :, None] == jnp.arange(experts, dtype=jnp.int32)[None, None, :]
    dense_gates = jnp.sum(jnp.where(named, gate_weights[:, :, None], 0.0), axis=1)
    kept_part = lax.reduce_precision(dense_gates, exponent_bits=8, mantissa_bits=7)
    upper = kept_part.astype(jnp.bfloat16)
    lower = (dense_gates - kept_part).astype(jnp.bfloat16)
    spare = -(2 * experts) % 128
    tail = jnp.concatenate([upper, lower, jnp.zeros((tok_count, spare), jnp.bfloat16)], axis=1)
    tail_width = tail.shape[1]
    payload = jnp.concatenate([moe_rows, tail], axis=1)
    lane = jnp.arange(tail_width, dtype=jnp.int32)
    own_lane = ((lane == place) | (lane == place + experts)).astype(jnp.float32)[None, :]
    payload = after(payload, own_lane)

    att_rows = lengths.shape[0]
    rope_rows = q_rope.reshape(att_rows, q_latent.shape[1], rope_cache.shape[1])
    att_half = att_rows // 2

    matrices = (w_gate[0], w_up[0], w_down[0])

    def attend(start, count, key):
        return attend_rows(q_latent, key, latent_cache, rope_cache, lengths, start, count)

    def pieces(c):
        return payload[c * chunk : (c + 1) * chunk]

    def along(mine):
        return [mine] + [send(mine, "z", k) for k in range(1, depth)]

    early = attend(0, att_half, rope_rows)
    gathered = []
    coming = along(pieces(0))
    coming[1] = after(coming[1], early)
    last = None
    for c in range(chunk_count):
        line = jnp.concatenate(coming, axis=0)
        if c + 1 < chunk_count:
            coming = along(after(pieces(c + 1), line))
        first = [line] + [send(line, "first", k) for k in range(1, side)]
        if c == 0:
            late = attend(att_half, att_half, after(rope_rows, line))
            first[1] = after(first[1], late, *coming)
        blocks = list(first)
        for k in range(1, side):
            blocks += [send(part, "last", k) for part in first]
        last = blocks[-1]
        gathered.append(blocks + [send(part, "role") for part in blocks])

    finished = []
    summed = None
    for c in range(chunk_count):
        half = len(gathered[c]) // 2
        own, other = gathered[c][:half], gathered[c][half:]
        if summed is not None:
            other = [after(other[0], *summed)] + other[1:]

        def expert(blocks):
            results = []
            for at in range(0, half, 4):
                results += expert_blocks(blocks[at : at + 4], *matrices, own_lane)
            return results

        other_results = expert(other)
        theirs = [send(part, "role") for part in other_results]
        if summed is not None:
            own = [after(own[0], other_results[-1])] + own[1:]
        if c + 1 < chunk_count:
            following = gathered[c + 1]
            own = [after(own[0], following[1], following[side], *theirs)] + own[1:]
        mine = expert(own)
        whole = [a.astype(jnp.float32) + b.astype(jnp.float32) for a, b in zip(mine, theirs)]
        whole = [whole[k * side : (k + 1) * side] for k in range(side)]
        sent = [[part.astype(jnp.bfloat16) for part in row] for row in whole]
        summed = sum(sent, [])
        kept = {}
        for a in reversed(range(side)):
            total = whole[0][a]
            for k in range(1, side):
                total = total + send(sent[k][a], "last", k).astype(jnp.float32)
            kept[a] = total
        total = kept[0]
        for k in range(1, side):
            total = total + send(kept[k].astype(jnp.bfloat16), "first", k).astype(jnp.float32)
        line = total.astype(jnp.bfloat16).reshape(depth, chunk, width)
        total = line[0].astype(jnp.float32)
        for k in range(1, depth):
            total = total + send(line[k], "z", k).astype(jnp.float32)
        finished.append(total.astype(jnp.bfloat16))
    moe_out = jnp.concatenate(finished, axis=0)
    attended = jnp.concatenate([early, late], axis=0)
    return (moe_out, attended)


def solution(mesh):
    placed = (
        P(("role", "dev"), None),
        P(("role", "dev"), None),
        P(("role", "dev"), None),
        P("dev", None, "role"),
        P("dev", None, "role"),
        P("dev", None, "role"),
        P(("role", "dev"), None, None),
        P(("role", "dev"), None),
        P(("role", "dev"), None, None),
        P(("role", "dev"), None, None),
        P(("role", "dev")),
    )
    return jax.shard_map(
        per_device,
        mesh=mesh,
        in_specs=placed,
        out_specs=(P(("role", "dev"), None), P(("role", "dev"), None, None)),
        check_vma=False,
    )
```

```python
import functools

import jax
import jax.numpy as jnp
from jax import lax
from jax.experimental import pallas as pl
from jax.experimental.pallas import tpu as pltpu
from jax.sharding import PartitionSpec as P

score_scale = 192.0 ** (-0.5)
both_axes = ("role", "dev")
chunk_count = 2


def shift_pairs(kind, step, depth, side):
    pairs = []
    for r in range(2):
        for z in range(depth):
            for y in range(side):
                for x in range(side):
                    to_r, to_z, to_y, to_x = r, z, y, x
                    if kind == "role":
                        to_r = 1 - r
                    elif kind == "z":
                        to_z = z ^ step
                    elif (kind == "first") == (r == 0):
                        to_y = y ^ step
                    else:
                        to_x = x ^ step
                    here = ((r * depth + z) * side + y) * side + x
                    there = ((to_r * depth + to_z) * side + to_y) * side + to_x
                    pairs.append((here, there))
    return pairs


def attend_kernel(lengths_ref, lat_ref, rope_ref, cache_ref, keys_ref, out_ref):
    length = lengths_ref[pl.program_id(0)]
    cache = cache_ref[0]
    scores = lax.dot_general(
        lat_ref[0], cache, (((1,), (1,)), ((), ())), preferred_element_type=jnp.float32
    )
    scores = scores + jnp.dot(rope_ref[0], keys_ref[0], preferred_element_type=jnp.float32)
    scores = scores * score_scale
    valid = lax.broadcasted_iota(jnp.int32, scores.shape, 1) < length
    scores = jnp.where(valid, scores, jnp.float32(-1e30))
    highest = jnp.max(scores, axis=1, keepdims=True)
    weights = jnp.where(valid, jnp.exp(scores - highest), jnp.float32(0.0))
    probs = weights * (1.0 / jnp.sum(weights, axis=1, keepdims=True))
    out_ref[0] = jnp.dot(
        probs.astype(jnp.bfloat16), cache, preferred_element_type=jnp.float32
    ).astype(jnp.bfloat16)


def attend_rows(q_latent, q_rope, latent_cache, rope_cache, lengths, start, count):
    heads, latent = q_latent.shape[1:]
    cached = latent_cache.shape[1]
    rope = rope_cache.shape[1]

    def spec(*shape):
        return pl.BlockSpec((1, *shape), lambda at, lengths_ref: (start + at, 0, 0))

    return pl.pallas_call(
        attend_kernel,
        out_shape=jax.ShapeDtypeStruct((count, heads, latent), jnp.bfloat16),
        grid_spec=pltpu.PrefetchScalarGridSpec(
            num_scalar_prefetch=1,
            grid=(count,),
            in_specs=[
                spec(heads, latent),
                spec(heads, rope),
                spec(cached, latent),
                spec(rope, cached),
            ],
            out_specs=pl.BlockSpec((1, heads, latent), lambda at, lengths_ref: (at, 0, 0)),
        ),
        compiler_params=pltpu.CompilerParams(vmem_limit_bytes=48 * 1024 * 1024),
        cost_estimate=pl.CostEstimate(
            flops=2 * count * heads * cached * (2 * latent + rope),
            bytes_accessed=2 * count * cached * (latent + rope),
            transcendentals=count * heads * cached,
        ),
        name="attend_rows",
    )(lengths[start : start + count], q_latent, q_rope, latent_cache, rope_cache)


def expert_kernel(count, lane_ref, *refs):
    blocks, refs = refs[:count], refs[count:]
    (gate_mat, up_mat, down_mat), refs = refs[:3], refs[3:]
    results, (hidden,) = refs[:count], refs[count:]
    block = blocks[0].shape[0]
    width, units = gate_mat.shape
    tile, slab = units // 2, width // 2
    chosen = jnp.concatenate([rows[:, :width] for rows in blocks], axis=0)
    tails = jnp.concatenate([rows[:, width:] for rows in blocks], axis=0)
    row_gates = jnp.sum(tails.astype(jnp.float32) * lane_ref[...], axis=1, keepdims=True)
    for piece in range(2):
        lanes = pl.ds(piece * tile, tile)
        gate_part = jnp.dot(chosen, gate_mat[:, lanes], preferred_element_type=jnp.float32)
        up_part = jnp.dot(chosen, up_mat[:, lanes], preferred_element_type=jnp.float32)
        silu = gate_part / (1.0 + jnp.exp(-gate_part))
        hidden[:, lanes] = (silu * up_part).astype(jnp.bfloat16)
    for piece in range(2):
        lanes = pl.ds(piece * slab, slab)
        result = lax.dot_general(
            hidden[...],
            down_mat[lanes, :],
            (((1,), (1,)), ((), ())),
            preferred_element_type=jnp.float32,
        )
        result = (result * row_gates).astype(jnp.bfloat16)
        for at in range(count):
            results[at][:, lanes] = result[at * block : (at + 1) * block]


def expert_blocks(blocks, gate_matrix, up_matrix, down_matrix, own_lane):
    count = len(blocks)
    block = blocks[0].shape[0]
    width, units = gate_matrix.shape
    total = count * block
    inside = pl.BlockSpec(memory_space=pltpu.VMEM)
    return pl.pallas_call(
        functools.partial(expert_kernel, count),
        out_shape=[jax.ShapeDtypeStruct((block, width), jnp.bfloat16)] * count,
        in_specs=[inside] * (count + 4),
        out_specs=[inside] * count,
        scratch_shapes=[pltpu.VMEM((total, units), jnp.bfloat16)],
        compiler_params=pltpu.CompilerParams(vmem_limit_bytes=10 * 1024 * 1024),
        cost_estimate=pl.CostEstimate(
            flops=6 * total * width * units,
            bytes_accessed=6 * width * units + 4 * total * width,
            transcendentals=total * units,
        ),
        name="expert_blocks",
    )(own_lane, *blocks, gate_matrix, up_matrix, down_matrix)


def after(value, *earlier):
    return lax.optimization_barrier((value, *earlier))[0]


def per_device(
    moe_rows,
    expert_ids,
    gate_weights,
    w_gate,
    w_up,
    w_down,
    q_latent,
    q_rope,
    latent_cache,
    rope_cache,
    lengths,
):
    tok_count, width = moe_rows.shape
    experts = lax.axis_size("dev")
    side = 1
    while experts % (4 * side * side) == 0 and (2 * side) ** 2 * 4 <= experts:
        side *= 2
    depth = experts // (side * side)
    chunk = tok_count // chunk_count

    def send(value, kind, step=1):
        return lax.ppermute(value, both_axes, shift_pairs(kind, step, depth, side))

    place = lax.axis_index("dev")
    named = expert_ids[:, :, None] == jnp.arange(experts, dtype=jnp.int32)[None, None, :]
    dense_gates = jnp.sum(jnp.where(named, gate_weights[:, :, None], 0.0), axis=1)
    kept_part = lax.reduce_precision(dense_gates, exponent_bits=8, mantissa_bits=7)
    upper = kept_part.astype(jnp.bfloat16)
    lower = (dense_gates - kept_part).astype(jnp.bfloat16)
    spare = -(2 * experts) % 128
    tail = jnp.concatenate([upper, lower, jnp.zeros((tok_count, spare), jnp.bfloat16)], axis=1)
    tail_width = tail.shape[1]
    payload = jnp.concatenate([moe_rows, tail], axis=1)
    lane = jnp.arange(tail_width, dtype=jnp.int32)
    own_lane = ((lane == place) | (lane == place + experts)).astype(jnp.float32)[None, :]
    payload = after(payload, own_lane)

    att_rows = lengths.shape[0]
    rope_rows = q_rope.reshape(att_rows, q_latent.shape[1], rope_cache.shape[1])
    att_half = att_rows // 2

    matrices = (w_gate[0], w_up[0], w_down[0])

    def attend(start, count, key):
        return attend_rows(q_latent, key, latent_cache, rope_cache, lengths, start, count)

    def pieces(c):
        return payload[c * chunk : (c + 1) * chunk]

    def along(mine):
        return [mine] + [send(mine, "z", k) for k in range(1, depth)]

    early = attend(0, att_half, rope_rows)
    gathered = []
    coming = along(pieces(0))
    coming[1] = after(coming[1], early)
    for c in range(chunk_count):
        line = jnp.concatenate(coming, axis=0)
        if c + 1 < chunk_count:
            coming = along(after(pieces(c + 1), line))
        first = [line] + [send(line, "first", k) for k in range(1, side)]
        if c == 0:
            late = attend(att_half, att_half, after(rope_rows, line))
            first[1] = after(first[1], late, *coming)
        blocks = list(first)
        for k in range(1, side):
            blocks += [send(part, "last", k) for part in first]
        gathered.append(blocks + [send(part, "role") for part in blocks])

    finished = []
    summed = None
    for c in range(chunk_count):
        half = len(gathered[c]) // 2
        own, other = gathered[c][:half], gathered[c][half:]
        if summed is not None:
            other = [after(other[0], *summed)] + other[1:]

        def expert(blocks):
            results = []
            for at in range(0, half, 4):
                results += expert_blocks(blocks[at : at + 4], *matrices, own_lane)
            return results

        other_results = expert(other)
        theirs = [send(part, "role") for part in other_results]
        if summed is not None:
            own = [after(own[0], theirs[-1])] + own[1:]
        if c + 1 < chunk_count:
            following = gathered[c + 1]
            own = [after(own[0], following[1], following[side], *theirs)] + own[1:]
        mine = expert(own)
        whole = [a.astype(jnp.float32) + b.astype(jnp.float32) for a, b in zip(mine, theirs)]
        whole = [whole[k * side : (k + 1) * side] for k in range(side)]
        sent = [[part.astype(jnp.bfloat16) for part in row] for row in whole]
        summed = sum(sent, [])
        kept = {}
        for a in reversed(range(side)):
            total = whole[0][a]
            for k in range(1, side):
                total = total + send(sent[k][a], "last", k).astype(jnp.float32)
            kept[a] = total
        total = kept[0]
        for k in range(1, side):
            total = total + send(kept[k].astype(jnp.bfloat16), "first", k).astype(jnp.float32)
        line = total.astype(jnp.bfloat16).reshape(depth, chunk, width)
        total = line[0].astype(jnp.float32)
        for k in range(1, depth):
            total = total + send(line[k], "z", k).astype(jnp.float32)
        finished.append(total.astype(jnp.bfloat16))
    moe_out = jnp.concatenate(finished, axis=0)
    attended = jnp.concatenate([early, late], axis=0)
    return (moe_out, attended)


def solution(mesh):
    placed = (
        P(("role", "dev"), None),
        P(("role", "dev"), None),
        P(("role", "dev"), None),
        P("dev", None, "role"),
        P("dev", None, "role"),
        P("dev", None, "role"),
        P(("role", "dev"), None, None),
        P(("role", "dev"), None),
        P(("role", "dev"), None, None),
        P(("role", "dev"), None, None),
        P(("role", "dev")),
    )
    return jax.shard_map(
        per_device,
        mesh=mesh,
        in_specs=placed,
        out_specs=(P(("role", "dev"), None), P(("role", "dev"), None, None)),
        check_vma=False,
    )
```

```python
import functools

import jax
import jax.numpy as jnp
from jax import lax
from jax.experimental import pallas as pl
from jax.experimental.pallas import tpu as pltpu
from jax.sharding import PartitionSpec as P

score_scale = 192.0 ** (-0.5)
both_axes = ("role", "dev")
chunk_count = 2


def shift_pairs(kind, step, depth, side):
    pairs = []
    for r in range(2):
        for z in range(depth):
            for y in range(side):
                for x in range(side):
                    to_r, to_z, to_y, to_x = r, z, y, x
                    if kind == "role":
                        to_r = 1 - r
                    elif kind == "z":
                        to_z = z ^ step
                    elif (kind == "first") == (r == 0):
                        to_y = y ^ step
                    else:
                        to_x = x ^ step
                    here = ((r * depth + z) * side + y) * side + x
                    there = ((to_r * depth + to_z) * side + to_y) * side + to_x
                    pairs.append((here, there))
    return pairs


def attend_kernel(lengths_ref, lat_ref, rope_ref, cache_ref, keys_ref, out_ref):
    length = lengths_ref[pl.program_id(0)]
    cache = cache_ref[0]
    scores = lax.dot_general(
        lat_ref[0], cache, (((1,), (1,)), ((), ())), preferred_element_type=jnp.float32
    )
    scores = scores + jnp.dot(rope_ref[0], keys_ref[0], preferred_element_type=jnp.float32)
    scores = scores * score_scale
    valid = lax.broadcasted_iota(jnp.int32, scores.shape, 1) < length
    scores = jnp.where(valid, scores, jnp.float32(-1e30))
    highest = jnp.max(scores, axis=1, keepdims=True)
    weights = jnp.where(valid, jnp.exp(scores - highest), jnp.float32(0.0))
    probs = weights * (1.0 / jnp.sum(weights, axis=1, keepdims=True))
    out_ref[0] = jnp.dot(
        probs.astype(jnp.bfloat16), cache, preferred_element_type=jnp.float32
    ).astype(jnp.bfloat16)


def attend_rows(q_latent, q_rope, latent_cache, rope_cache, lengths, start, count):
    heads, latent = q_latent.shape[1:]
    cached = latent_cache.shape[1]
    rope = rope_cache.shape[1]

    def spec(*shape):
        return pl.BlockSpec((1, *shape), lambda at, lengths_ref: (start + at, 0, 0))

    return pl.pallas_call(
        attend_kernel,
        out_shape=jax.ShapeDtypeStruct((count, heads, latent), jnp.bfloat16),
        grid_spec=pltpu.PrefetchScalarGridSpec(
            num_scalar_prefetch=1,
            grid=(count,),
            in_specs=[
                spec(heads, latent),
                spec(heads, rope),
                spec(cached, latent),
                spec(rope, cached),
            ],
            out_specs=pl.BlockSpec((1, heads, latent), lambda at, lengths_ref: (at, 0, 0)),
        ),
        compiler_params=pltpu.CompilerParams(vmem_limit_bytes=48 * 1024 * 1024),
        cost_estimate=pl.CostEstimate(
            flops=2 * count * heads * cached * (2 * latent + rope),
            bytes_accessed=2 * count * cached * (latent + rope),
            transcendentals=count * heads * cached,
        ),
        name="attend_rows",
    )(lengths[start : start + count], q_latent, q_rope, latent_cache, rope_cache)


def expert_kernel(count, lane_ref, *refs):
    blocks, refs = refs[:count], refs[count:]
    (gate_mat, up_mat, down_mat), refs = refs[:3], refs[3:]
    results, (hidden,) = refs[:count], refs[count:]
    block = blocks[0].shape[0]
    width, units = gate_mat.shape
    tile, slab = units // 2, width // 2
    chosen = jnp.concatenate([rows[:, :width] for rows in blocks], axis=0)
    tails = jnp.concatenate([rows[:, width:] for rows in blocks], axis=0)
    row_gates = jnp.sum(tails.astype(jnp.float32) * lane_ref[...], axis=1, keepdims=True)
    for piece in range(2):
        lanes = pl.ds(piece * tile, tile)
        gate_part = jnp.dot(chosen, gate_mat[:, lanes], preferred_element_type=jnp.float32)
        up_part = jnp.dot(chosen, up_mat[:, lanes], preferred_element_type=jnp.float32)
        silu = gate_part / (1.0 + jnp.exp(-gate_part))
        hidden[:, lanes] = (silu * up_part).astype(jnp.bfloat16)
    for piece in range(2):
        lanes = pl.ds(piece * slab, slab)
        result = lax.dot_general(
            hidden[...],
            down_mat[lanes, :],
            (((1,), (1,)), ((), ())),
            preferred_element_type=jnp.float32,
        )
        result = (result * row_gates).astype(jnp.bfloat16)
        for at in range(count):
            results[at][:, lanes] = result[at * block : (at + 1) * block]


def expert_blocks(blocks, gate_matrix, up_matrix, down_matrix, own_lane):
    count = len(blocks)
    block = blocks[0].shape[0]
    width, units = gate_matrix.shape
    total = count * block
    inside = pl.BlockSpec(memory_space=pltpu.VMEM)
    return pl.pallas_call(
        functools.partial(expert_kernel, count),
        out_shape=[jax.ShapeDtypeStruct((block, width), jnp.bfloat16)] * count,
        in_specs=[inside] * (count + 4),
        out_specs=[inside] * count,
        scratch_shapes=[pltpu.VMEM((total, units), jnp.bfloat16)],
        compiler_params=pltpu.CompilerParams(vmem_limit_bytes=10 * 1024 * 1024),
        cost_estimate=pl.CostEstimate(
            flops=6 * total * width * units,
            bytes_accessed=6 * width * units + 4 * total * width,
            transcendentals=total * units,
        ),
        name="expert_blocks",
    )(own_lane, *blocks, gate_matrix, up_matrix, down_matrix)


def pack_kernel(experts, rows_ref, ids_ref, gates_ref, *payload_refs):
    count, width = rows_ref.shape
    chunk = payload_refs[0].shape[0]
    tail_width = payload_refs[0].shape[1] - width
    lane = lax.broadcasted_iota(jnp.int32, (tail_width, count), 0)
    named = jnp.where(lane < experts, lane, lane - experts)
    dense = jnp.zeros((tail_width, count), jnp.float32)
    for k in range(ids_ref.shape[0]):
        dense = jnp.where(ids_ref[k : k + 1, :] == named, gates_ref[k : k + 1, :], dense)
    upper = dense.astype(jnp.bfloat16).astype(jnp.float32)
    tail = jnp.where(lane < experts, upper, dense - upper).T.astype(jnp.bfloat16)
    for at, payload_ref in enumerate(payload_refs):
        payload_ref[:, :width] = rows_ref[at * chunk : (at + 1) * chunk]
        payload_ref[:, width:] = tail[at * chunk : (at + 1) * chunk]


def pack_rows(rows, ids, gates, experts, tail_width):
    count, width = rows.shape
    chunk = count // chunk_count
    inside = pl.BlockSpec(memory_space=pltpu.VMEM)
    return pl.pallas_call(
        functools.partial(pack_kernel, experts),
        out_shape=[jax.ShapeDtypeStruct((chunk, width + tail_width), rows.dtype)] * chunk_count,
        in_specs=[inside] * 3,
        out_specs=[inside] * chunk_count,
        name="pack_rows",
    )(rows, ids.T, gates.T)


def after(value, *earlier):
    return lax.optimization_barrier((value, *earlier))[0]


def per_device(
    moe_rows,
    expert_ids,
    gate_weights,
    w_gate,
    w_up,
    w_down,
    q_latent,
    q_rope,
    latent_cache,
    rope_cache,
    lengths,
):
    tok_count, width = moe_rows.shape
    experts = lax.axis_size("dev")
    side = 1
    while experts % (4 * side * side) == 0 and (2 * side) ** 2 * 4 <= experts:
        side *= 2
    depth = experts // (side * side)
    chunk = tok_count // chunk_count

    def send(value, kind, step=1):
        return lax.ppermute(value, both_axes, shift_pairs(kind, step, depth, side))

    place = lax.axis_index("dev")
    tail_width = -(-2 * experts // 128) * 128
    payloads = list(pack_rows(moe_rows, expert_ids, gate_weights, experts, tail_width))
    lane = jnp.arange(tail_width, dtype=jnp.int32)
    own_lane = ((lane == place) | (lane == place + experts)).astype(jnp.float32)[None, :]
    payloads[0] = after(payloads[0], own_lane)

    att_rows = lengths.shape[0]
    rope_rows = q_rope.reshape(att_rows, q_latent.shape[1], rope_cache.shape[1])
    att_half = att_rows // 2

    matrices = (w_gate[0], w_up[0], w_down[0])

    def attend(start, count, key):
        return attend_rows(q_latent, key, latent_cache, rope_cache, lengths, start, count)

    def pieces(c):
        return payloads[c]

    def along(mine):
        return [mine] + [send(mine, "z", k) for k in range(1, depth)]

    early = attend(0, att_half, rope_rows)
    gathered = []
    coming = along(pieces(0))
    coming[1] = after(coming[1], early)
    for c in range(chunk_count):
        line = jnp.concatenate(coming, axis=0)
        if c + 1 < chunk_count:
            coming = along(after(pieces(c + 1), line))
        first = [line] + [send(line, "first", k) for k in range(1, side)]
        if c == 0:
            late = attend(att_half, att_half, after(rope_rows, line))
            first[1] = after(first[1], late, *coming)
        blocks = list(first)
        for k in range(1, side):
            blocks += [send(part, "last", k) for part in first]
        gathered.append(blocks + [send(part, "role") for part in blocks])

    finished = []
    summed = None
    for c in range(chunk_count):
        half = len(gathered[c]) // 2
        own, other = gathered[c][:half], gathered[c][half:]
        if summed is not None:
            other = [after(other[0], *summed)] + other[1:]

        def expert(blocks):
            results = []
            for at in range(0, half, 4):
                results += expert_blocks(blocks[at : at + 4], *matrices, own_lane)
            return results

        other_results = expert(other)
        theirs = [send(part, "role") for part in other_results]
        if summed is not None:
            own = [after(own[0], theirs[-1])] + own[1:]
        if c + 1 < chunk_count:
            following = gathered[c + 1]
            own = [after(own[0], following[1], following[side], *theirs)] + own[1:]
        mine = expert(own)
        whole = [a.astype(jnp.float32) + b.astype(jnp.float32) for a, b in zip(mine, theirs)]
        whole = [whole[k * side : (k + 1) * side] for k in range(side)]
        sent = [[part.astype(jnp.bfloat16) for part in row] for row in whole]
        summed = sum(sent, [])
        kept = {}
        for a in reversed(range(side)):
            total = whole[0][a]
            for k in range(1, side):
                total = total + send(sent[k][a], "last", k).astype(jnp.float32)
            kept[a] = total
        total = kept[0]
        for k in range(1, side):
            total = total + send(kept[k].astype(jnp.bfloat16), "first", k).astype(jnp.float32)
        line = total.astype(jnp.bfloat16).reshape(depth, chunk, width)
        total = line[0].astype(jnp.float32)
        for k in range(1, depth):
            total = total + send(line[k], "z", k).astype(jnp.float32)
        finished.append(total.astype(jnp.bfloat16))
    moe_out = jnp.concatenate(finished, axis=0)
    attended = jnp.concatenate([early, late], axis=0)
    return (moe_out, attended)


def solution(mesh):
    placed = (
        P(("role", "dev"), None),
        P(("role", "dev"), None),
        P(("role", "dev"), None),
        P("dev", None, "role"),
        P("dev", None, "role"),
        P("dev", None, "role"),
        P(("role", "dev"), None, None),
        P(("role", "dev"), None),
        P(("role", "dev"), None, None),
        P(("role", "dev"), None, None),
        P(("role", "dev")),
    )
    return jax.shard_map(
        per_device,
        mesh=mesh,
        in_specs=placed,
        out_specs=(P(("role", "dev"), None), P(("role", "dev"), None, None)),
        check_vma=False,
    )
```
